512 devices in a mesh: seq: 128 (over z, y, core), rep: 4 (over x).
Axes of the slice: x: 4, y: 4, z: 16, core: 2. Of those that a mesh axis runs over, the one named last changes fastest.
Arguments:
- points: bfloat16 [4, 131072, 128], P('rep', 'seq'), may hold values from -6 to 6
- grad_rows: bfloat16 [4, 131072, 128], P('rep', 'seq'), may hold values from -6 to 6
- order: int32 [4, 131072], P('rep', 'seq'), may hold values from 0 to 131071, as said below
- w_qkv: bfloat16 [128, 384], replicated, may hold values from -0.5 to 0.5
- w_out: bfloat16 [128, 128], replicated, may hold values from -0.5 to 0.5
- norm_gain: float32 [128], replicated, may hold values from 0.5 to 1.5
- conv_taps: float32 [7, 128], replicated, may hold values from -1.5 to 1.5
Outputs:
- grad_points: float32 [4, 131072, 128], P('rep', 'seq')
- grad_qkv: float32 [128, 384], replicated
- grad_wout: float32 [128, 128], replicated
- grad_gain: float32 [128], replicated
- grad_taps: float32 [7, 128], replicated
The draws below stay inside these ranges and needn't reach their ends.
Inputs may be any that keep to these rules, and one draw needn't show every extreme that they name: Within each slab, order is a permutation of 0 to 131071. Take aligned blocks of 1024 points and of 1024 positions. The blocks of points map one to one onto the blocks of positions (each block of points has its own block of positions): each block of points sends exactly 4 rows to every other block of positions and its remaining 1024 - 127 * 4 rows to its own.
All inputs are finite; a program needn't handle non-finite values.
Results may differ from the reference program's by a relative error of at most 0.0075.
The reference program's roundings to bfloat16 on the way count: a program that leaves them out, or rounds other values in their place, can miss the bound.
Values may be sent and summed in bfloat16 or wider, within the bound.
A program may use at most 64 MiB of HBM per device.

```python
import jax
import jax.numpy as jnp
from jax import lax

D = 128
HEADS = 8
PATCH = 1024
RADIUS = 3
TOK_DEV = 1024
SPILL = 4
TOKENS = 131072
REPS = 4


def draw_order(key, part):
    shards = TOKENS // TOK_DEV
    spread_rows = (shards - 1) * SPILL

    def one_slab(slab_key):
        first, second, third = jax.random.split(slab_key, 3)
        mains = jax.random.permutation(first, shards).astype(jnp.int32)
        owner_of = jnp.zeros((shards,), jnp.int32).at[mains].set(jnp.arange(shards, dtype=jnp.int32))
        bases = jnp.arange(shards, dtype=jnp.int32)[:, None] * TOK_DEV
        positions = jax.vmap(lambda k: jax.random.permutation(k, TOK_DEV))(jax.random.split(second, shards)).astype(jnp.int32) + bases
        block_ids = jnp.arange(shards, dtype=jnp.int32)
        lane = jnp.arange(SPILL, dtype=jnp.int32)

        def one_block(point_block):
            main = mains[point_block]
            step = (point_block - owner_of + shards) % shards
            index = jnp.maximum(step - 1, 0)[:, None] * SPILL + lane[None, :]
            picked = jnp.take_along_axis(positions, index, axis=1)
            keys = (block_ids == main).astype(jnp.int32)
            ordering = jnp.argsort(keys, stable=True)
            spread = picked[ordering].reshape(shards * SPILL)[:spread_rows]
            own = positions[main][spread_rows:]
            return jnp.concatenate([own, spread])
        values = jax.vmap(one_block)(block_ids)
        rows = jax.vmap(lambda k: jax.random.permutation(k, TOK_DEV))(jax.random.split(third, shards)).astype(jnp.int32)

        def place(row_ids, vals):
            return jnp.zeros((TOK_DEV,), jnp.int32).at[row_ids].set(vals)
        return jax.vmap(place)(rows, values).reshape(TOKENS)
    return jax.vmap(one_slab)(jax.random.split(key, REPS))


def shard_levels(key, shape, cuts, least, top_value):
    def one(position, parts):
        draws = jax.random.uniform(jax.random.fold_in(jax.random.fold_in(key, 6), position), (parts,), jnp.float32, least / len(cuts), top_value / len(cuts))
        return jnp.repeat(jnp.exp(draws), shape[position] // parts).reshape((-1,) + (1,) * (len(shape) - position - 1))

    gain = one(*cuts[0])
    for cut in cuts[1:]:
        gain = gain * one(*cut)
    return gain


def noise(rng, dims, scale, limit, cuts=(), kind=jnp.bfloat16):
    entries = jax.random.normal(rng, dims, jnp.float32) * scale
    if len(cuts) > 0:
        entries = shard_levels(rng, dims, cuts, -0.22, 0.18) * entries
    return jnp.clip(entries, min=-limit, max=limit).astype(kind)


def setup_inputs(seed: int = 0) -> dict:
    key_list = jax.random.split(jax.random.key(seed), 8)
    return {
        "points": noise(key_list[0], (REPS, TOKENS, D), 1.0, 6.0, ((0, 4), (1, 128))),
        "grad_rows": noise(key_list[1], (REPS, TOKENS, D), 1.0, 6.0, ((0, 4), (1, 128))),
        "order": draw_order(jax.random.fold_in(key_list[7], 71), 0),
        "w_qkv": noise(key_list[3], (D, 3 * D), D ** -0.5, 0.5),
        "w_out": noise(key_list[4], (D, D), D ** -0.5, 0.5),
        "norm_gain": jnp.clip(1.0 + 0.1 * jax.random.normal(key_list[5], (D,), jnp.float32), 0.5, 1.5),
        "conv_taps": noise(key_list[6], (2 * RADIUS + 1, D), 0.3, 1.5, (), jnp.float32),
    }


def head_attend(query, keyset, values):
    scale = 1.0 / jnp.sqrt(jnp.float32(query.shape[1]))
    scores = jnp.einsum('qe,ke->qk', query, keyset, preferred_element_type=jnp.float32) * scale
    scores = scores - lax.optimization_barrier(jnp.max(scores, axis=1, keepdims=True))
    expon = jnp.exp(scores)
    probs = (expon / lax.optimization_barrier(jnp.sum(expon, axis=1, keepdims=True))).astype(jnp.bfloat16)
    return jnp.einsum('qk,ke->qe', probs, values, preferred_element_type=jnp.float32).astype(jnp.bfloat16)

def layer_forward(rows, w_qkv, w_out, norm_gain):
    count, width = rows.shape
    center = rows - lax.optimization_barrier(jnp.mean(rows, axis=1, keepdims=True))
    spread = lax.optimization_barrier(jnp.mean(center * center, axis=1, keepdims=True))
    normed = center * lax.rsqrt(spread + 1e-05) * norm_gain
    mixed = jnp.dot(normed.astype(jnp.bfloat16), w_qkv.astype(jnp.bfloat16), preferred_element_type=jnp.float32)
    split_heads = mixed.astype(jnp.bfloat16).reshape(count, 3, HEADS, width // HEADS).transpose(1, 2, 0, 3)
    attend_one = jax.checkpoint(lambda triple: head_attend(triple[0], triple[1], triple[2]))
    attended = lax.map(attend_one, (split_heads[0], split_heads[1], split_heads[2]))
    attended = attended.transpose(1, 0, 2).reshape(count, width)
    return rows + jnp.dot(attended, w_out.astype(jnp.bfloat16), preferred_element_type=jnp.float32)

def patch_grads(rows, cotangent, w_qkv, w_out, norm_gain):
    primal, pull = jax.vjp(layer_forward, rows.astype(jnp.float32), w_qkv.astype(jnp.float32), w_out.astype(jnp.float32), norm_gain)
    return pull(cotangent.astype(jnp.float32))

def patch_sweep(patched, patch_grad, w_qkv, w_out, norm_gain):
    width = patched.shape[1]
    blocks = patched.reshape(-1, PATCH, width)
    cot_blocks = patch_grad.reshape(-1, PATCH, width)
    start = (jnp.zeros(w_qkv.shape, jnp.float32), jnp.zeros(w_out.shape, jnp.float32), jnp.zeros(norm_gain.shape, jnp.float32))

    def advance(carry, pair):
        grads = patch_grads(pair[0], pair[1], w_qkv, w_out, norm_gain)
        carry = (carry[0] + grads[1], carry[1] + grads[2], carry[2] + grads[3])
        return (carry, grads[0].astype(jnp.bfloat16))
    totals, backs = lax.scan(advance, start, (blocks, cot_blocks))
    return (totals, backs.reshape(-1, width))

def reference(points, grad_rows, order, w_qkv, w_out, norm_gain, conv_taps):
    taps = conv_taps.shape[0]
    reach = taps // 2
    total_qkv = jnp.zeros(w_qkv.shape, jnp.float32)
    total_out = jnp.zeros(w_out.shape, jnp.float32)
    total_gain = jnp.zeros(norm_gain.shape, jnp.float32)
    total_taps = jnp.zeros(conv_taps.shape, jnp.float32)
    grads_all = []
    for slab in range(points.shape[0]):
        feats = points[slab].astype(jnp.float32)
        count = feats.shape[0]
        padded = jnp.pad(feats, ((reach, reach), (0, 0)))
        encoded = feats
        for offset in range(taps):
            encoded = encoded + conv_taps[offset] * padded[offset:offset + count]
        encoded = encoded.astype(jnp.bfloat16)
        slots = order[slab]
        patched = jnp.zeros(encoded.shape, jnp.bfloat16).at[slots].set(encoded)
        patch_grad = jnp.zeros(encoded.shape, jnp.bfloat16).at[slots].set(grad_rows[slab])
        totals, backs = patch_sweep(patched, patch_grad, w_qkv, w_out, norm_gain)
        total_qkv = total_qkv + totals[0]
        total_out = total_out + totals[1]
        total_gain = total_gain + totals[2]
        curve_back = backs[slots].astype(jnp.float32)
        back_pad = jnp.pad(curve_back, ((reach, reach), (0, 0)))
        grad_feats = curve_back
        for offset in range(taps):
            grad_feats = grad_feats + conv_taps[offset] * back_pad[2 * reach - offset:2 * reach - offset + count]
        tap_terms = jnp.stack([lax.optimization_barrier(jnp.sum(curve_back * padded[offset:offset + count], axis=0)) for offset in range(taps)])
        total_taps = total_taps + tap_terms
        grads_all.append(grad_feats)
    return (jnp.stack(grads_all), total_qkv, total_out, total_gain, total_taps)
```

```python
import functools

import jax
import jax.numpy as jnp
from jax import lax
from jax.experimental import pallas as pl
from jax.experimental.pallas import tpu as pltpu
from jax.sharding import PartitionSpec as P

F32 = jnp.float32
BF = jnp.bfloat16
MESH = pl.DeviceIdType.MESH
HEADS = 8
HALF = 512
ROWS = 1024
WIDTH = 128
NZ = 16
NYC = 8
NX = 4
NW = NX * NYC
SEQ = NZ * NYC


def dot(a, b):
    return jnp.dot(a, b, preferred_element_type=F32)


def ntdot(a, b):
    return lax.dot_general(a, b, (((1,), (1,)), ((), ())), preferred_element_type=F32)


def iota(shape, dim):
    return lax.broadcasted_iota(jnp.int32, shape, dim)


def hot(cond):
    return jnp.where(cond, 1.0, 0.0).astype(BF)


def kernel(
    pts_ref, cot_ref, order_ref, wqkv_ref, wout_ref, gain_ref, taps_ref,
    gp_ref, gq_ref, gw_ref, gg_ref, gt_ref,
    pp, pb, pbt, pret, q4, mine, agz, agw, scot, senc,
    tx, rx, bt, rr, patch, cotp,
    qT, kT, vT, doT, kf, vf, attT, dqT, dkT, dvT, xhT, rs, nbT, sbuf, eb, xb, w1, mref,
    cpad, acc, rsb, part, zb, full, fin, tmine, tw, tsum, tz,
    ssem, rsem,
):
    me = lax.axis_index("seq")
    rep = lax.axis_index("rep")
    z = me // NYC
    yc = lax.rem(me, NYC)
    w = rep * NYC + yc
    sig = yc * NZ + z

    def z_peer(t):
        zz = lax.rem(z + 1 + t, NZ)
        return zz, (zz * NYC + yc, rep)

    def yc_peer(t):
        cc = lax.rem(yc + 1 + t, NYC)
        return cc, (z * NYC + cc, rep)

    def w_peer(t):
        ww = lax.rem(w + 1 + t, NW)
        return ww, (z * NYC + lax.rem(ww, NYC), ww // NYC)

    def seq_peer(t):
        dd = lax.rem(me + 1 + t, SEQ)
        return lax.rem(dd, NYC) * NZ + dd // NYC, (dd, rep)

    nxt = (lax.rem(me + 1, SEQ), rep)
    prv = (lax.rem(me + SEQ - 1, SEQ), rep)

    def push(src, dst, k, dev):
        pltpu.make_async_remote_copy(
            src_ref=src, dst_ref=dst, send_sem=ssem.at[k], recv_sem=rsem.at[k],
            device_id=dev, device_id_type=MESH,
        ).start()

    def loop(count, step):
        def body(t, carry):
            step(t)
            return carry

        lax.fori_loop(0, count, body, 0)

    def wait_in(ref, k):
        pltpu.make_async_copy(ref, ref, rsem.at[k]).wait()

    def wait_out(ref, k):
        pltpu.make_async_copy(ref, ref, ssem.at[k]).wait()

    barrier = pltpu.get_barrier_semaphore()

    def greet(dev):
        pl.semaphore_signal(barrier, inc=1, device_id=dev, device_id_type=MESH)

    loop(NZ - 1, lambda t: greet(z_peer(t)[1]))
    loop(NW - 1, lambda t: greet(w_peer(t)[1]))
    greet(nxt)
    greet(prv)

    pp[8 : 8 + ROWS, :] = pts_ref[0].astype(F32)
    dest = order_ref[...] // ROWS
    blocks = iota((SEQ, ROWS), 0)
    hits = jnp.where(blocks == dest, 1.0, 0.0)
    counts = jnp.sum(hits, axis=1, keepdims=True)
    is_main = jnp.where(counts > 4.5, 1.0, 0.0)
    main = jnp.sum(is_main * iota((SEQ, 1), 0).astype(F32), axis=0, keepdims=True)
    mine[...] = jnp.broadcast_to(main, (1, WIDTH))
    pb[...] = hot(iota((ROWS, ROWS), 0) < iota((ROWS, ROWS), 1))
    before = dot(hits.astype(BF), pb[...])
    rank = jnp.sum(hits * before, axis=0, keepdims=True)
    main_row = jnp.sum(hits * is_main, axis=0, keepdims=True)
    slot = jnp.where(
        (main_row > 0.5) & (rank > 3.5),
        rank + float(HALF - 4),
        dest.astype(F32) * 4.0 + rank,
    )
    pb[...] = hot(iota((ROWS, ROWS), 0).astype(F32) == slot)
    slot_col = jnp.broadcast_to(slot, (8, ROWS)).T[:, 0:1]
    pbt[...] = hot(iota((ROWS, ROWS), 1).astype(F32) == slot_col)
    scot[...] = dot(pb[...], cot_ref[0]).astype(BF)
    eye = hot(iota((WIDTH, WIDTH), 0) == iota((WIDTH, WIDTH), 1))
    wq = wqkv_ref[...]
    wqT = jnp.concatenate(
        [wq[:, j * WIDTH : (j + 1) * WIDTH].astype(F32).T.astype(BF) for j in range(3)], axis=0
    )

    pl.semaphore_wait(barrier, NZ - 1 + NW - 1 + 2)

    def send_z(t):
        push(mine, agz.at[z], 0, z_peer(t)[1])

    loop(NZ - 1, send_z)
    push(pp.at[pl.ds(ROWS, 8)], pp.at[pl.ds(0, 8)], 1, nxt)
    push(pp.at[pl.ds(8, 8)], pp.at[pl.ds(ROWS + 8, 8)], 2, prv)
    agz[z] = mine[...]
    wait_in(agz.at[pl.ds(0, NZ - 1)], 0)

    def send_yc(t):
        push(agz, agw.at[yc], 3, yc_peer(t)[1])

    loop(NYC - 1, send_yc)
    agw[yc] = agz[...]
    wait_in(pp.at[pl.ds(0, 8)], 1)
    wait_in(pp.at[pl.ds(ROWS + 8, 8)], 2)
    has_prev = jnp.where(me > 0, 1.0, 0.0)
    has_next = jnp.where(me < SEQ - 1, 1.0, 0.0)
    wait_out(pp.at[pl.ds(ROWS, 8)], 1)
    wait_out(pp.at[pl.ds(8, 8)], 2)
    pp[0:8, :] = pp[0:8, :] * has_prev
    pp[ROWS + 8 : ROWS + 16, :] = pp[ROWS + 8 : ROWS + 16, :] * has_next
    enc = pp[8 : 8 + ROWS, :]
    for t in range(7):
        enc = enc + taps_ref[t : t + 1, :] * pp[5 + t : 5 + t + ROWS, :]
    senc[...] = dot(pb[...], enc.astype(BF)).astype(BF)
    wait_in(agw.at[pl.ds(0, NYC - 1)], 3)
    owners = agw[...].reshape(SEQ, WIDTH)
    pick = hot(owners == iota((SEQ, WIDTH), 1).astype(F32))
    grow = hot(iota((HALF, SEQ), 0) // 4 == iota((HALF, SEQ), 1))
    wide = ntdot(dot(grow, pick).astype(BF), grow)
    same = (iota((HALF, HALF), 0) % 4) == (iota((HALF, HALF), 1) % 4)
    q4[...] = jnp.where(same, wide, 0.0).astype(BF)
    tx[:, 0:4, :] = dot(q4[...], senc[0:HALF, :]).astype(BF).reshape(SEQ, 4, WIDTH)
    tx[:, 4:8, :] = dot(q4[...], scot[0:HALF, :]).astype(BF).reshape(SEQ, 4, WIDTH)

    def send_rows(t):
        slot_of, dev = seq_peer(t)
        push(tx.at[slot_of], rx.at[sig], 4, dev)

    loop(SEQ - 1, send_rows)
    rx[sig] = tx[sig]
    pret[...] = ntdot(pbt[:, 0:HALF], q4[...]).astype(BF)
    patch[HALF:, :] = senc[HALF:, :]
    cotp[HALF:, :] = scot[HALF:, :]
    gain = gain_ref[...]
    gainc = jnp.sum(jnp.where(eye.astype(F32) > 0.5, gain, 0.0), axis=1, keepdims=True)
    wait_in(rx.at[pl.ds(0, SEQ - 1)], 4)
    patch[0:HALF, :] = rx[:, 0:4, :].reshape(HALF, WIDTH)
    cotp[0:HALF, :] = rx[:, 4:8, :].reshape(HALF, WIDTH)

    xT = ntdot(eye, patch[...])
    center = xT - jnp.mean(xT, axis=0, keepdims=True)
    r = lax.rsqrt(jnp.mean(center * center, axis=0, keepdims=True) + 1e-5)
    xh = center * r
    xhT[...] = xh
    rs[...] = jnp.broadcast_to(r, rs.shape)
    nT = (xh * gainc).astype(BF)
    nbT[...] = nT
    mixed = dot(wqT, nT)
    qkvT = mixed.astype(BF)
    qT[...] = qkvT[0:128] * jnp.asarray(0.25, BF)
    kT[...] = qkvT[128:256]
    vT[...] = qkvT[256:384]
    kf[...] = mixed[128:256].T.astype(BF)
    vf[...] = mixed[256:384].T.astype(BF)
    doT[...] = ntdot(wout_ref[...], cotp[...]).astype(BF)
    ones = jnp.ones((16, ROWS), BF)
    for h in range(HEADS):
        w1[h * 48 : h * 48 + 16, :] = qkvT[256 + h * 16 : 272 + h * 16]
        w1[h * 48 + 16 : h * 48 + 32, :] = ones
        w1[h * 48 + 32 : h * 48 + 48, :] = qkvT[128 + h * 16 : 144 + h * 16]
    head_of = iota((WIDTH, ROWS), 0) // 16

    def masked(ref, h):
        return jnp.where(head_of == h, ref[...].astype(F32), 0.0).astype(BF)

    first = dot(kf[...], masked(qT, 0))
    sbuf[0] = first
    mref[0] = jnp.broadcast_to(jnp.max(first, axis=0, keepdims=True), (8, ROWS))

    def head(h, cur, other, last):
        hs = pl.ds(pl.multiple_of(h * 16, 16), 16)
        if not last:
            q_next = masked(qT, h + 1)
        do_wide = masked(doT, h)
        top = mref[cur][0:1, :]
        top_next = None
        for c in range(4):
            ks = slice(c * 256, c * 256 + 256)
            if not last:
                s = dot(kf[ks, :], q_next)
                sbuf[other, ks, :] = s
                high = jnp.max(s, axis=0, keepdims=True)
                top_next = high if top_next is None else jnp.maximum(top_next, high)
            e = jnp.exp(sbuf[cur, ks, :] - top)
            t = dot(vf[ks, :], do_wide)
            eb[ks, :] = e.astype(BF)
            xb[ks, :] = (e * t).astype(BF)
        if not last:
            mref[other] = jnp.broadcast_to(top_next, (8, ROWS))
        a = dot(w1[pl.ds(pl.multiple_of(h * 48, 16), 48), :], eb[...])
        inv = 1.0 / a[16:17]
        o = a[0:16] * inv
        attT[hs, :] = o.astype(BF)
        kx = dot(kT[hs, :], xb[...])
        do = doT[hs, :].astype(F32)
        q = qT[hs, :].astype(F32)
        delta = jnp.sum(do * o, axis=0, keepdims=True)
        dqT[hs, :] = ((kx - delta * a[32:48]) * (inv * 0.25)).astype(BF)
        back = ntdot(jnp.concatenate([do * inv, q * (-delta * inv)], axis=0).astype(BF), eb[...])
        dk = ntdot((q * inv).astype(BF), xb[...])
        dvT[hs, :] = back[0:16].astype(BF)
        dkT[hs, :] = (dk + back[16:32]).astype(BF)

    def pair(i, carry):
        head(2 * i, 0, 1, False)
        head(2 * i + 1, 1, 0, False)
        return carry

    lax.fori_loop(0, HEADS // 2 - 1, pair, 0)
    head(HEADS - 2, 0, 1, False)
    head(HEADS - 1, 1, 0, True)

    dall = jnp.concatenate([dqT[...], dkT[...], dvT[...]], axis=0)
    dnT = dot(wq, dall).astype(BF).astype(F32)
    xh = xhT[...]
    dxh = dnT * gainc
    m1 = jnp.mean(dxh, axis=0, keepdims=True)
    m2 = jnp.mean(dxh * xh, axis=0, keepdims=True)
    dxT = (dxh - m1 - xh * m2) * rs[0:1, :]
    patch[...] = (dxT.T + cotp[...].astype(F32)).astype(BF)
    bt[...] = patch[0:HALF, :].reshape(SEQ, 4, WIDTH)

    def send_back(t):
        slot_of, dev = seq_peer(t)
        push(bt.at[slot_of], rr.at[sig], 5, dev)

    loop(SEQ - 1, send_back)
    rr[sig] = bt[sig]

    ggT = jnp.sum(dnT * xh, axis=1, keepdims=True)
    gain_row = jnp.sum(jnp.where(eye.astype(F32) > 0.5, ggT, 0.0), axis=0, keepdims=True)
    for j in range(3):
        acc[j * 8 : j * 8 + 8] = ntdot(nbT[...], dall[j * WIDTH : (j + 1) * WIDTH]).reshape(8, 16, WIDTH)
    acc[24:32] = dot(attT[...], cotp[...]).reshape(8, 16, WIDTH)

    def send_part(t):
        ww, dev = w_peer(t)
        push(acc.at[ww], rsb.at[w], 6, dev)

    loop(NW - 1, send_part)
    rsb[w] = acc[w]
    own = dot(pbt[:, HALF:], patch[HALF:, :])
    wait_in(rsb.at[pl.ds(0, NW - 1)], 6)
    part[...] = jnp.sum(rsb[...], axis=0)

    def send_part_z(t):
        push(part, zb.at[z], 7, z_peer(t)[1])

    loop(NZ - 1, send_part_z)
    zb[z] = part[...]

    wait_in(rr.at[pl.ds(0, SEQ - 1)], 5)
    cb = own + dot(pret[...], rr[...].reshape(HALF, WIDTH))
    cpad[8 : 8 + ROWS, :] = cb
    push(cpad.at[pl.ds(ROWS, 8)], cpad.at[pl.ds(0, 8)], 8, nxt)
    push(cpad.at[pl.ds(8, 8)], cpad.at[pl.ds(ROWS + 8, 8)], 9, prv)
    tap_rows = [jnp.sum(cb * pp[5 + t : 5 + t + ROWS, :], axis=0, keepdims=True) for t in range(7)]
    tmine[...] = jnp.concatenate(tap_rows + [gain_row], axis=0)

    def send_tap(t):
        push(tmine, tw.at[w], 10, w_peer(t)[1])

    loop(NW - 1, send_tap)
    tw[w] = tmine[...]

    wait_in(zb.at[pl.ds(0, NZ - 1)], 7)
    full[...] = jnp.sum(zb[...], axis=0)

    def send_full(t):
        push(full, fin.at[w], 11, w_peer(t)[1])

    loop(NW - 1, send_full)
    fin[w] = full[...]

    wait_in(tw.at[pl.ds(0, NW - 1)], 10)
    tsum[...] = jnp.sum(tw[...], axis=0)

    def send_tap_z(t):
        push(tsum, tz.at[z], 12, z_peer(t)[1])

    loop(NZ - 1, send_tap_z)
    tz[z] = tsum[...]

    wait_in(cpad.at[pl.ds(0, 8)], 8)
    wait_in(cpad.at[pl.ds(ROWS + 8, 8)], 9)
    wait_out(cpad.at[pl.ds(ROWS, 8)], 8)
    wait_out(cpad.at[pl.ds(8, 8)], 9)
    cpad[0:8, :] = cpad[0:8, :] * has_prev
    cpad[ROWS + 8 : ROWS + 16, :] = cpad[ROWS + 8 : ROWS + 16, :] * has_next
    res = cpad[8 : 8 + ROWS, :]
    for t in range(7):
        res = res + taps_ref[t : t + 1, :] * cpad[11 - t : 11 - t + ROWS, :]
    gp_ref[0] = res

    wait_in(fin.at[pl.ds(0, NW - 1)], 11)
    for j in range(3):
        gq_ref[:, j * WIDTH : (j + 1) * WIDTH] = fin[j * 8 : j * 8 + 8].reshape(WIDTH, WIDTH)
    gw_ref[...] = fin[24:32].reshape(WIDTH, WIDTH)
    wait_in(tz.at[pl.ds(0, NZ - 1)], 12)
    total = jnp.sum(tz[...], axis=0)
    gt_ref[...] = total[0:7]
    gg_ref[...] = total[7:8]

    wait_out(agz.at[pl.ds(0, NZ - 1)], 0)
    wait_out(agw.at[pl.ds(0, NYC - 1)], 3)
    wait_out(rx.at[pl.ds(0, SEQ - 1)], 4)
    wait_out(rr.at[pl.ds(0, SEQ - 1)], 5)
    wait_out(rsb.at[pl.ds(0, NW - 1)], 6)
    wait_out(zb.at[pl.ds(0, NZ - 1)], 7)
    wait_out(tw.at[pl.ds(0, NW - 1)], 10)
    wait_out(fin.at[pl.ds(0, NW - 1)], 11)
    wait_out(tz.at[pl.ds(0, NZ - 1)], 12)


def body(points, grad_rows, order, w_qkv, w_out, norm_gain, conv_taps):
    def vm(shape, dtype):
        return pltpu.VMEM(shape, dtype)

    sq = (ROWS, ROWS)
    wide = (WIDTH, ROWS)
    tall = (ROWS, WIDTH)
    scratch = [
        vm((ROWS + 16, WIDTH), F32), vm(sq, BF), vm(sq, BF), vm((ROWS, HALF), BF), vm((HALF, HALF), BF),
        vm((1, WIDTH), F32), vm((NZ, 1, WIDTH), F32), vm((NYC, NZ, 1, WIDTH), F32), vm(tall, BF), vm(tall, BF),
        vm((SEQ, 8, WIDTH), BF), vm((SEQ, 8, WIDTH), BF), vm((SEQ, 4, WIDTH), BF), vm((SEQ, 4, WIDTH), BF),
        vm(tall, BF), vm(tall, BF),
        vm(wide, BF), vm(wide, BF), vm(wide, BF), vm(wide, BF), vm(tall, BF), vm(tall, BF),
        vm(wide, BF), vm(wide, BF), vm(wide, BF), vm(wide, BF), vm(wide, F32), vm((8, ROWS), F32), vm(wide, BF),
        vm((2,) + sq, F32), vm(sq, BF), vm(sq, BF), vm((HEADS * 48, ROWS), BF), vm((2, 8, ROWS), F32),
        vm((ROWS + 16, WIDTH), F32), vm((NW, 16, WIDTH), F32), vm((NW, 16, WIDTH), F32), vm((16, WIDTH), F32),
        vm((NZ, 16, WIDTH), F32), vm((16, WIDTH), F32), vm((NW, 16, WIDTH), F32),
        vm((8, WIDTH), F32), vm((NW, 8, WIDTH), F32), vm((8, WIDTH), F32), vm((NZ, 8, WIDTH), F32),
        pltpu.SemaphoreType.DMA((13,)), pltpu.SemaphoreType.DMA((13,)),
    ]
    spec = pl.BlockSpec(memory_space=pltpu.VMEM)
    shape = jax.ShapeDtypeStruct
    gp, gq, gw, gg, gt = pl.pallas_call(
        kernel,
        out_shape=(
            shape((1, ROWS, WIDTH), F32), shape((WIDTH, 3 * WIDTH), F32), shape((WIDTH, WIDTH), F32),
            shape((1, WIDTH), F32), shape((7, WIDTH), F32),
        ),
        in_specs=[spec] * 7,
        out_specs=[spec] * 5,
        scratch_shapes=scratch,
        compiler_params=pltpu.CompilerParams(
            collective_id=0, has_side_effects=True, vmem_limit_bytes=56 * 2**20
        ),
    )(points, grad_rows, order, w_qkv, w_out, norm_gain.reshape(1, WIDTH), conv_taps)
    return gp, gq, gw, gg.reshape(WIDTH), gt


def solution(mesh):
    placed = (P("rep", "seq", None), P("rep", "seq", None), P("rep", "seq"), P(), P(), P(), P())
    return jax.shard_map(
        body,
        mesh=mesh,
        in_specs=placed,
        out_specs=(P("rep", "seq", None), P(), P(), P(), P()),
        check_vma=False,
    )
```

```python
import functools

import jax
import jax.numpy as jnp
from jax import lax
from jax.experimental import pallas as pl
from jax.experimental.pallas import tpu as pltpu
from jax.sharding import PartitionSpec as P

F32 = jnp.float32
BF = jnp.bfloat16
MESH = pl.DeviceIdType.MESH
HEADS = 8
HALF = 512
ROWS = 1024
WIDTH = 128
NZ = 16
NYC = 8
NX = 4
NW = NX * NYC
SEQ = NZ * NYC


def dot(a, b):
    return jnp.dot(a, b, preferred_element_type=F32)


def ntdot(a, b):
    return lax.dot_general(a, b, (((1,), (1,)), ((), ())), preferred_element_type=F32)


def iota(shape, dim):
    return lax.broadcasted_iota(jnp.int32, shape, dim)


def hot(cond):
    return jnp.where(cond, 1.0, 0.0).astype(BF)


def kernel(
    pts_ref, cot_ref, order_ref, wqkv_ref, wout_ref, gain_ref, taps_ref,
    curve_ref, sums_ref, small_ref,
    pp, pb, pbt, pret, q4, mine, agz, agw, scot, senc,
    tx, rx, c0, c1, c2, bt, rr, patch, cotp,
    qT, kT, vT, doT, kf, vf, attT, dqT, dkT, dvT, xhT, rs, nbT, sbuf, eb, xb, w1, mref,
    oT, keT, invs,
    cpad, acc, rsb, part, zb, full, fin, tmine, tw, tsum, tz,
    ssem, rsem,
):
    me = lax.axis_index("seq")
    rep = lax.axis_index("rep")
    z = me // NYC
    yc = lax.rem(me, NYC)
    w = rep * NYC + yc
    sig = yc * NZ + z

    def z_peer(t):
        zz = lax.rem(z + 1 + t, NZ)
        return zz, (zz * NYC + yc, rep)

    def yc_peer(t):
        cc = lax.rem(yc + 1 + t, NYC)
        return cc, (z * NYC + cc, rep)

    def w_peer(t):
        ww = lax.rem(w + 1 + t, NW)
        return ww, (z * NYC + lax.rem(ww, NYC), ww // NYC)

    def seq_peer(t):
        dd = lax.rem(me + 1 + t, SEQ)
        return lax.rem(dd, NYC) * NZ + dd // NYC, (dd, rep)

    nxt = (lax.rem(me + 1, SEQ), rep)
    prv = (lax.rem(me + SEQ - 1, SEQ), rep)

    def push(src, dst, k, dev):
        pltpu.make_async_remote_copy(
            src_ref=src, dst_ref=dst, send_sem=ssem.at[k], recv_sem=rsem.at[k],
            device_id=dev, device_id_type=MESH,
        ).start()

    def loop(count, step):
        def body(t, carry):
            step(t)
            return carry

        lax.fori_loop(0, count, body, 0)

    def wait_in(ref, k):
        pltpu.make_async_copy(ref, ref, rsem.at[k]).wait()

    def wait_out(ref, k):
        pltpu.make_async_copy(ref, ref, ssem.at[k]).wait()

    barrier = pltpu.get_barrier_semaphore()

    def greet(dev):
        pl.semaphore_signal(barrier, inc=1, device_id=dev, device_id_type=MESH)

    loop(NZ - 1, lambda t: greet(z_peer(t)[1]))
    loop(NYC - 1, lambda t: greet(yc_peer(t)[1]))
    loop(NX - 1, lambda t: greet((me, lax.rem(rep + 1 + t, NX))))
    greet(nxt)
    greet(prv)

    pp[8 : 8 + ROWS, :] = pts_ref[0].astype(F32)
    dest = order_ref[...] // ROWS
    blocks = iota((SEQ, ROWS), 0)
    hits = jnp.where(blocks == dest, 1.0, 0.0)
    counts = jnp.sum(hits, axis=1, keepdims=True)
    is_main = jnp.where(counts > 4.5, 1.0, 0.0)
    main = jnp.sum(is_main * iota((SEQ, 1), 0).astype(F32), axis=0, keepdims=True)
    mine[...] = jnp.broadcast_to(main, (1, WIDTH))
    pb[...] = hot(iota((ROWS, ROWS), 0) < iota((ROWS, ROWS), 1))
    before = dot(hits.astype(BF), pb[...])
    rank = jnp.sum(hits * before, axis=0, keepdims=True)
    main_row = jnp.sum(hits * is_main, axis=0, keepdims=True)
    slot = jnp.where(
        (main_row > 0.5) & (rank > 3.5),
        rank + float(HALF - 4),
        dest.astype(F32) * 4.0 + rank,
    )
    pb[...] = hot(iota((ROWS, ROWS), 0).astype(F32) == slot)
    slot_col = jnp.broadcast_to(slot, (8, ROWS)).T[:, 0:1]
    pbt[...] = hot(iota((ROWS, ROWS), 1).astype(F32) == slot_col)
    scot[...] = dot(pb[...], cot_ref[0]).astype(BF)
    eye = hot(iota((WIDTH, WIDTH), 0) == iota((WIDTH, WIDTH), 1))
    wq = wqkv_ref[...]
    wqT = jnp.concatenate(
        [wq[:, j * WIDTH : (j + 1) * WIDTH].astype(F32).T.astype(BF) for j in range(3)], axis=0
    )

    pl.semaphore_wait(barrier, NZ - 1 + NYC - 1 + NX - 1 + 2)

    def send_z(t):
        push(mine, agz.at[z], 0, z_peer(t)[1])

    loop(NZ - 1, send_z)
    push(pp.at[pl.ds(ROWS, 8)], pp.at[pl.ds(0, 8)], 1, nxt)
    push(pp.at[pl.ds(8, 8)], pp.at[pl.ds(ROWS + 8, 8)], 2, prv)
    agz[z] = mine[...]
    wait_in(pp.at[pl.ds(0, 8)], 1)
    wait_in(pp.at[pl.ds(ROWS + 8, 8)], 2)
    has_prev = jnp.where(me > 0, 1.0, 0.0)
    has_next = jnp.where(me < SEQ - 1, 1.0, 0.0)
    wait_out(pp.at[pl.ds(ROWS, 8)], 1)
    wait_out(pp.at[pl.ds(8, 8)], 2)
    pp[0:8, :] = pp[0:8, :] * has_prev
    pp[ROWS + 8 : ROWS + 16, :] = pp[ROWS + 8 : ROWS + 16, :] * has_next
    enc = pp[8 : 8 + ROWS, :]
    for t in range(7):
        enc = enc + taps_ref[t : t + 1, :] * pp[5 + t : 5 + t + ROWS, :]
    senc[...] = dot(pb[...], enc.astype(BF)).astype(BF)
    wait_in(agz.at[pl.ds(0, NZ - 1)], 0)

    def send_yc(t):
        push(agz, agw.at[yc], 3, yc_peer(t)[1])

    loop(NYC - 1, send_yc)
    agw[yc] = agz[...]
    wait_in(agw.at[pl.ds(0, NYC - 1)], 3)
    owners = agw[...].reshape(SEQ, WIDTH)
    pick = hot(owners == iota((SEQ, WIDTH), 1).astype(F32))
    grow = hot(iota((HALF, SEQ), 0) // 4 == iota((HALF, SEQ), 1))
    wide = ntdot(dot(grow, pick).astype(BF), grow)
    same = (iota((HALF, HALF), 0) % 4) == (iota((HALF, HALF), 1) % 4)
    q4[...] = jnp.where(same, wide, 0.0).astype(BF)
    tx[...] = dot(q4[...], senc[0:HALF, :]).astype(BF).reshape(SEQ, 4, WIDTH)

    def send_rows(t):
        slot_of, dev = seq_peer(t)
        push(tx.at[slot_of], rx.at[sig], 4, dev)

    loop(SEQ - 1, send_rows)
    rx[sig] = tx[sig]
    c0[...] = dot(q4[...], scot[0:HALF, :]).astype(BF).reshape(NYC, NZ, 4, WIDTH)

    def send_cot(t):
        cc, dev = yc_peer(t)
        push(c0.at[cc], c1.at[yc], 13, dev)

    loop(NYC - 1, send_cot)
    c1[yc] = c0[yc]
    pret[...] = ntdot(pbt[:, 0:HALF], q4[...]).astype(BF)
    patch[HALF:, :] = senc[HALF:, :]
    cotp[HALF:, :] = scot[HALF:, :]
    gain = gain_ref[...]
    gainc = jnp.sum(jnp.where(eye.astype(F32) > 0.5, gain, 0.0), axis=1, keepdims=True)
    wait_in(c1.at[pl.ds(0, NYC - 1)], 13)
    wait_in(rx.at[pl.ds(0, SEQ - 1)], 4)

    def send_cot_z(t):
        zz, dev = z_peer(t)
        push(c1.at[:, zz], c2.at[:, z], 14, dev)

    loop(NZ - 1, send_cot_z)
    c2[:, z] = c1[:, z]
    patch[0:HALF, :] = rx[...].reshape(HALF, WIDTH)

    xT = ntdot(eye, patch[...])
    center = xT - jnp.mean(xT, axis=0, keepdims=True)
    r = lax.rsqrt(jnp.mean(center * center, axis=0, keepdims=True) + 1e-5)
    xh = center * r
    xhT[...] = xh
    rs[...] = jnp.broadcast_to(r, rs.shape)
    nT = (xh * gainc).astype(BF)
    nbT[...] = nT
    mixed = dot(wqT, nT)
    qkvT = mixed.astype(BF)
    qT[...] = qkvT[0:128] * jnp.asarray(0.25, BF)
    kT[...] = qkvT[128:256]
    vT[...] = qkvT[256:384]
    kf[...] = mixed[128:256].T.astype(BF)
    vf[...] = mixed[256:384].T.astype(BF)
    ones = jnp.ones((16, ROWS), BF)
    for h in range(HEADS):
        w1[h * 48 : h * 48 + 16, :] = qkvT[256 + h * 16 : 272 + h * 16]
        w1[h * 48 + 16 : h * 48 + 32, :] = ones
        w1[h * 48 + 32 : h * 48 + 48, :] = qkvT[128 + h * 16 : 144 + h * 16]
    head_of = iota((WIDTH, ROWS), 0) // 16

    def masked(ref, h):
        return jnp.where(head_of == h, ref[...].astype(F32), 0.0).astype(BF)

    first = dot(kf[...], masked(qT, 0))
    sbuf[0] = first
    mref[0] = jnp.broadcast_to(jnp.max(first, axis=0, keepdims=True), (8, ROWS))

    def forward(h, cur, other, last):
        hs = pl.ds(pl.multiple_of(h * 16, 16), 16)
        if not last:
            q_next = masked(qT, h + 1)
        top = mref[cur][0:1, :]
        top_next = None
        for c in range(4):
            ks = slice(c * 256, c * 256 + 256)
            if not last:
                s = dot(kf[ks, :], q_next)
                sbuf[other, ks, :] = s
                high = jnp.max(s, axis=0, keepdims=True)
                top_next = high if top_next is None else jnp.maximum(top_next, high)
            eb[h, ks, :] = jnp.exp(sbuf[cur, ks, :] - top).astype(BF)
        if not last:
            mref[other] = jnp.broadcast_to(top_next, (8, ROWS))
        a = dot(w1[pl.ds(pl.multiple_of(h * 48, 16), 48), :], eb[h])
        inv = 1.0 / a[16:17]
        o = a[0:16] * inv
        attT[hs, :] = o.astype(BF)
        oT[hs, :] = o
        keT[hs, :] = a[32:48]
        invs[h] = jnp.broadcast_to(inv, (8, ROWS))

    def backward(h):
        hs = pl.ds(pl.multiple_of(h * 16, 16), 16)
        do_wide = masked(doT, h)
        for c in range(4):
            ks = slice(c * 256, c * 256 + 256)
            t = dot(vf[ks, :], do_wide)
            xb[ks, :] = (eb[h, ks, :].astype(F32) * t).astype(BF)
        inv = invs[h][0:1, :]
        do = doT[hs, :].astype(F32)
        q = qT[hs, :].astype(F32)
        delta = jnp.sum(do * oT[hs, :], axis=0, keepdims=True)
        back = ntdot(jnp.concatenate([do * inv, q * (-delta * inv)], axis=0).astype(BF), eb[h])
        kx = dot(kT[hs, :], xb[...])
        dqT[hs, :] = ((kx - delta * keT[hs, :]) * (inv * 0.25)).astype(BF)
        dk = ntdot((q * inv).astype(BF), xb[...])
        dvT[hs, :] = back[0:16].astype(BF)
        dkT[hs, :] = (dk + back[16:32]).astype(BF)

    def pair(i, carry):
        forward(2 * i, 0, 1, False)
        forward(2 * i + 1, 1, 0, False)
        return carry

    lax.fori_loop(0, HEADS // 2 - 1, pair, 0)
    forward(HEADS - 2, 0, 1, False)
    forward(HEADS - 1, 1, 0, True)

    wait_in(c2.at[:, pl.ds(0, NZ - 1)], 14)
    cotp[0:HALF, :] = c2[...].reshape(HALF, WIDTH)
    doT[...] = ntdot(wout_ref[...], cotp[...]).astype(BF)

    def back_head(h, carry):
        backward(h)
        return carry

    lax.fori_loop(0, HEADS, back_head, 0)

    dall = jnp.concatenate([dqT[...], dkT[...], dvT[...]], axis=0)
    dnT = dot(wq, dall).astype(BF).astype(F32)
    xh = xhT[...]
    dxh = dnT * gainc
    m1 = jnp.mean(dxh, axis=0, keepdims=True)
    m2 = jnp.mean(dxh * xh, axis=0, keepdims=True)
    dxT = (dxh - m1 - xh * m2) * rs[0:1, :]
    patch[...] = (dxT.T + cotp[...].astype(F32)).astype(BF)
    bt[...] = patch[0:HALF, :].reshape(SEQ, 4, WIDTH)

    for j in range(3):
        acc[j * 8 : j * 8 + 8] = ntdot(nbT[...], dall[j * WIDTH : (j + 1) * WIDTH]).reshape(8, 16, WIDTH)
    acc[24:32] = dot(attT[...], cotp[...]).reshape(8, 16, WIDTH)

    def send_part(t):
        ww, dev = w_peer(t)
        push(acc.at[ww], rsb.at[w], 6, dev)

    loop(NW - 1, send_part)
    rsb[w] = acc[w]

    def send_back(t):
        slot_of, dev = seq_peer(t)
        push(bt.at[slot_of], rr.at[sig], 5, dev)

    loop(SEQ - 1, send_back)
    rr[sig] = bt[sig]
    ggT = jnp.sum(dnT * xh, axis=1, keepdims=True)
    gain_row = jnp.sum(jnp.where(eye.astype(F32) > 0.5, ggT, 0.0), axis=0, keepdims=True)
    wait_in(rsb.at[pl.ds(0, NW - 1)], 6)
    part[...] = jnp.sum(rsb[...], axis=0)

    def send_part_z(t):
        push(part, zb.at[z], 7, z_peer(t)[1])

    loop(NZ - 1, send_part_z)
    zb[z] = part[...]
    own = dot(pbt[:, HALF:], patch[HALF:, :])

    wait_in(rr.at[pl.ds(0, SEQ - 1)], 5)
    cb = own + dot(pret[...], rr[...].reshape(HALF, WIDTH))
    cpad[8 : 8 + ROWS, :] = cb
    push(cpad.at[pl.ds(ROWS, 8)], cpad.at[pl.ds(0, 8)], 8, nxt)
    push(cpad.at[pl.ds(8, 8)], cpad.at[pl.ds(ROWS + 8, 8)], 9, prv)
    tap_rows = [jnp.sum(cb * pp[5 + t : 5 + t + ROWS, :], axis=0, keepdims=True) for t in range(7)]
    tmine[...] = jnp.concatenate(tap_rows + [gain_row], axis=0)

    def send_tap(t):
        push(tmine, tw.at[w], 10, w_peer(t)[1])

    loop(NW - 1, send_tap)
    tw[w] = tmine[...]
    curve_ref[16 : 16 + ROWS, :] = cb.astype(BF)

    wait_in(tw.at[pl.ds(0, NW - 1)], 10)
    tsum[...] = jnp.sum(tw[...], axis=0)

    def send_tap_z(t):
        push(tsum, tz.at[z], 12, z_peer(t)[1])

    loop(NZ - 1, send_tap_z)
    tz[z] = tsum[...]

    wait_in(zb.at[pl.ds(0, NZ - 1)], 7)
    full[...] = jnp.sum(zb[...], axis=0)

    def send_full(t):
        push(full, fin.at[w], 11, w_peer(t)[1])

    loop(NW - 1, send_full)
    fin[w] = full[...]

    wait_in(cpad.at[pl.ds(0, 8)], 8)
    wait_in(cpad.at[pl.ds(ROWS + 8, 8)], 9)
    wait_out(cpad.at[pl.ds(ROWS, 8)], 8)
    wait_out(cpad.at[pl.ds(8, 8)], 9)
    zero = jnp.zeros((8, WIDTH), F32)
    curve_ref[0:16, :] = jnp.concatenate([zero, cpad[0:8, :] * has_prev], axis=0).astype(BF)
    curve_ref[ROWS + 16 : ROWS + 32, :] = jnp.concatenate(
        [cpad[ROWS + 8 : ROWS + 16, :] * has_next, zero], axis=0
    ).astype(BF)

    wait_out(agz.at[pl.ds(0, NZ - 1)], 0)
    wait_out(agw.at[pl.ds(0, NYC - 1)], 3)
    wait_out(rx.at[pl.ds(0, SEQ - 1)], 4)
    wait_out(c1.at[pl.ds(0, NYC - 1)], 13)
    wait_out(c2.at[:, pl.ds(0, NZ - 1)], 14)
    wait_out(rr.at[pl.ds(0, SEQ - 1)], 5)
    wait_out(rsb.at[pl.ds(0, NW - 1)], 6)
    wait_out(zb.at[pl.ds(0, NZ - 1)], 7)
    wait_out(tw.at[pl.ds(0, NW - 1)], 10)
    wait_out(fin.at[pl.ds(0, NW - 1)], 11)
    wait_out(tz.at[pl.ds(0, NZ - 1)], 12)

    wait_in(fin.at[pl.ds(0, NW - 1)], 11)
    sums_ref[...] = fin[...].reshape(HALF, WIDTH)
    wait_in(tz.at[pl.ds(0, NZ - 1)], 12)
    small_ref[...] = jnp.sum(tz[...], axis=0)


def finish(curve_ref, sums_ref, small_ref, taps_ref, gp_ref, gq_ref, gw_ref, gg_ref, gt_ref, cpad):
    cpad[...] = curve_ref[...].astype(F32)
    res = cpad[16 : 16 + ROWS, :]
    for t in range(7):
        res = res + taps_ref[t : t + 1, :] * cpad[19 - t : 19 - t + ROWS, :]
    gp_ref[0] = res
    for j in range(3):
        gq_ref[:, j * WIDTH : (j + 1) * WIDTH] = sums_ref[j * WIDTH : (j + 1) * WIDTH, :]
    gw_ref[...] = sums_ref[3 * WIDTH :, :]
    gt_ref[...] = small_ref[0:7, :]
    gg_ref[...] = small_ref[7:8, :]


def body(points, grad_rows, order, w_qkv, w_out, norm_gain, conv_taps):
    def vm(shape, dtype):
        return pltpu.VMEM(shape, dtype)

    sq = (ROWS, ROWS)
    wide = (WIDTH, ROWS)
    tall = (ROWS, WIDTH)
    scratch = [
        vm((ROWS + 16, WIDTH), F32), vm(sq, BF), vm(sq, BF), vm((ROWS, HALF), BF), vm((HALF, HALF), BF),
        vm((1, WIDTH), F32), vm((NZ, 1, WIDTH), F32), vm((NYC, NZ, 1, WIDTH), F32), vm(tall, BF), vm(tall, BF),
        vm((SEQ, 4, WIDTH), BF), vm((SEQ, 4, WIDTH), BF),
        vm((NYC, NZ, 4, WIDTH), BF), vm((NYC, NZ, 4, WIDTH), BF), vm((NYC, NZ, 4, WIDTH), BF),
        vm((SEQ, 4, WIDTH), BF), vm((SEQ, 4, WIDTH), BF),
        vm(tall, BF), vm(tall, BF),
        vm(wide, BF), vm(wide, BF), vm(wide, BF), vm(wide, BF), vm(tall, BF), vm(tall, BF),
        vm(wide, BF), vm(wide, BF), vm(wide, BF), vm(wide, BF), vm(wide, F32), vm((8, ROWS), F32), vm(wide, BF),
        vm((2,) + sq, F32), vm((HEADS,) + sq, BF), vm(sq, BF), vm((HEADS * 48, ROWS), BF), vm((2, 8, ROWS), F32),
        vm(wide, F32), vm(wide, F32), vm((HEADS, 8, ROWS), F32),
        vm((ROWS + 16, WIDTH), F32), vm((NW, 16, WIDTH), F32), vm((NW, 16, WIDTH), F32), vm((16, WIDTH), F32),
        vm((NZ, 16, WIDTH), F32), vm((16, WIDTH), F32), vm((NW, 16, WIDTH), F32),
        vm((8, WIDTH), F32), vm((NW, 8, WIDTH), F32), vm((8, WIDTH), F32), vm((NZ, 8, WIDTH), F32),
        pltpu.SemaphoreType.DMA((15,)), pltpu.SemaphoreType.DMA((15,)),
    ]
    spec = pl.BlockSpec(memory_space=pltpu.VMEM)
    shape = jax.ShapeDtypeStruct
    curve, sums, small = pl.pallas_call(
        kernel,
        out_shape=(shape((ROWS + 32, WIDTH), BF), shape((HALF, WIDTH), F32), shape((8, WIDTH), F32)),
        in_specs=[spec] * 7,
        out_specs=[spec] * 3,
        scratch_shapes=scratch,
        compiler_params=pltpu.CompilerParams(
            collective_id=0, has_side_effects=True, vmem_limit_bytes=56 * 2**20
        ),
    )(points, grad_rows, order, w_qkv, w_out, norm_gain.reshape(1, WIDTH), conv_taps)
    gp, gq, gw, gg, gt = pl.pallas_call(
        finish,
        out_shape=(
            shape((1, ROWS, WIDTH), F32), shape((WIDTH, 3 * WIDTH), F32), shape((WIDTH, WIDTH), F32),
            shape((1, WIDTH), F32), shape((7, WIDTH), F32),
        ),
        in_specs=[spec] * 4,
        out_specs=[spec] * 5,
        scratch_shapes=[vm((ROWS + 32, WIDTH), F32)],
    )(curve, sums, small, conv_taps)
    return gp, gq, gw, gg.reshape(WIDTH), gt


def solution(mesh):
    placed = (P("rep", "seq", None), P("rep", "seq", None), P("rep", "seq"), P(), P(), P(), P())
    return jax.shard_map(
        body,
        mesh=mesh,
        in_specs=placed,
        out_specs=(P("rep", "seq", None), P(), P(), P(), P()),
        check_vma=False,
    )
```

```python
import functools

import jax
import jax.numpy as jnp
from jax import lax
from jax.experimental import pallas as pl
from jax.experimental.pallas import tpu as pltpu
from jax.sharding import PartitionSpec as P

F32 = jnp.float32
BF = jnp.bfloat16
MESH = pl.DeviceIdType.MESH
HEADS = 8
HALF = 512
ROWS = 1024
WIDTH = 128
NZ = 16
NYC = 8
NX = 4
NW = NX * NYC
SEQ = NZ * NYC


def dot(a, b):
    return jnp.dot(a, b, preferred_element_type=F32)


def ntdot(a, b):
    return lax.dot_general(a, b, (((1,), (1,)), ((), ())), preferred_element_type=F32)


def iota(shape, dim):
    return lax.broadcasted_iota(jnp.int32, shape, dim)


def hot(cond):
    return jnp.where(cond, 1.0, 0.0).astype(BF)


def kernel(
    pts_ref, cot_ref, order_ref, wqkv_ref, wout_ref, gain_ref, taps_ref,
    curve_ref, sums_ref, small_ref,
    pp, pown, pret, q4, mine, agz, agw, scot, senc,
    tx, rx, c0, c1, c2, bt, rr, patch, cotp,
    qT, kT, vT, doT, kf, vf, attT, dqT, dkT, dvT, xhT, rs, nbT, sbuf, eb, xb, w1, mref,
    oT, keT, invs,
    cpad, acc, rsb, part, zb, full, fin, tmine, tw, tsum, tz,
    ssem, rsem,
):
    me = lax.axis_index("seq")
    rep = lax.axis_index("rep")
    z = me // NYC
    yc = lax.rem(me, NYC)
    w = rep * NYC + yc
    sig = yc * NZ + z

    def z_peer(t):
        zz = lax.rem(z + 1 + t, NZ)
        return zz, (zz * NYC + yc, rep)

    def yc_peer(t):
        cc = lax.rem(yc + 1 + t, NYC)
        return cc, (z * NYC + cc, rep)

    def w_peer(t):
        ww = lax.rem(w + 1 + t, NW)
        return ww, (z * NYC + lax.rem(ww, NYC), ww // NYC)

    def seq_peer(t):
        dd = lax.rem(me + 1 + t, SEQ)
        return lax.rem(dd, NYC) * NZ + dd // NYC, (dd, rep)

    nxt = (lax.rem(me + 1, SEQ), rep)
    prv = (lax.rem(me + SEQ - 1, SEQ), rep)

    def push(src, dst, k, dev):
        pltpu.make_async_remote_copy(
            src_ref=src, dst_ref=dst, send_sem=ssem.at[k], recv_sem=rsem.at[k],
            device_id=dev, device_id_type=MESH,
        ).start()

    def loop(count, step):
        def body(t, carry):
            step(t)
            return carry

        lax.fori_loop(0, count, body, 0)

    def wait_in(ref, k):
        pltpu.make_async_copy(ref, ref, rsem.at[k]).wait()

    def wait_out(ref, k):
        pltpu.make_async_copy(ref, ref, ssem.at[k]).wait()

    barrier = pltpu.get_barrier_semaphore()
    pb = xb.at[0]
    pbt = xb.at[1]

    def greet(dev):
        pl.semaphore_signal(barrier, inc=1, device_id=dev, device_id_type=MESH)

    loop(NZ - 1, lambda t: greet(z_peer(t)[1]))
    loop(NYC - 1, lambda t: greet(yc_peer(t)[1]))
    loop(NX - 1, lambda t: greet((me, lax.rem(rep + 1 + t, NX))))
    greet(nxt)
    greet(prv)

    pp[8 : 8 + ROWS, :] = pts_ref[0].astype(F32)
    dest = order_ref[...] // ROWS
    blocks = iota((SEQ, ROWS), 0)
    hits = jnp.where(blocks == dest, 1.0, 0.0)
    counts = jnp.sum(hits, axis=1, keepdims=True)
    is_main = jnp.where(counts > 4.5, 1.0, 0.0)
    main = jnp.sum(is_main * iota((SEQ, 1), 0).astype(F32), axis=0, keepdims=True)
    mine[...] = jnp.broadcast_to(main, (1, WIDTH))
    pb[...] = hot(iota((ROWS, ROWS), 0) < iota((ROWS, ROWS), 1))
    before = dot(hits.astype(BF), pb[...])
    rank = jnp.sum(hits * before, axis=0, keepdims=True)
    main_row = jnp.sum(hits * is_main, axis=0, keepdims=True)
    slot = jnp.where(
        (main_row > 0.5) & (rank > 3.5),
        rank + float(HALF - 4),
        dest.astype(F32) * 4.0 + rank,
    )
    pb[...] = hot(iota((ROWS, ROWS), 0).astype(F32) == slot)
    slot_col = jnp.broadcast_to(slot, (8, ROWS)).T[:, 0:1]
    pbt[...] = hot(iota((ROWS, ROWS), 1).astype(F32) == slot_col)
    pown[...] = pbt[:, HALF:]
    scot[...] = dot(pb[...], cot_ref[0]).astype(BF)
    eye = hot(iota((WIDTH, WIDTH), 0) == iota((WIDTH, WIDTH), 1))
    wq = wqkv_ref[...]
    wqT = jnp.concatenate(
        [wq[:, j * WIDTH : (j + 1) * WIDTH].astype(F32).T.astype(BF) for j in range(3)], axis=0
    )

    pl.semaphore_wait(barrier, NZ - 1 + NYC - 1 + NX - 1 + 2)

    def send_z(t):
        push(mine, agz.at[z], 0, z_peer(t)[1])

    loop(NZ - 1, send_z)
    push(pp.at[pl.ds(ROWS, 8)], pp.at[pl.ds(0, 8)], 1, nxt)
    push(pp.at[pl.ds(8, 8)], pp.at[pl.ds(ROWS + 8, 8)], 2, prv)
    agz[z] = mine[...]
    wait_in(pp.at[pl.ds(0, 8)], 1)
    wait_in(pp.at[pl.ds(ROWS + 8, 8)], 2)
    has_prev = jnp.where(me > 0, 1.0, 0.0)
    has_next = jnp.where(me < SEQ - 1, 1.0, 0.0)
    wait_out(pp.at[pl.ds(ROWS, 8)], 1)
    wait_out(pp.at[pl.ds(8, 8)], 2)
    pp[0:8, :] = pp[0:8, :] * has_prev
    pp[ROWS + 8 : ROWS + 16, :] = pp[ROWS + 8 : ROWS + 16, :] * has_next
    enc = pp[8 : 8 + ROWS, :]
    for t in range(7):
        enc = enc + taps_ref[t : t + 1, :] * pp[5 + t : 5 + t + ROWS, :]
    senc[...] = dot(pb[...], enc.astype(BF)).astype(BF)
    wait_in(agz.at[pl.ds(0, NZ - 1)], 0)

    def send_yc(t):
        push(agz, agw.at[yc], 3, yc_peer(t)[1])

    loop(NYC - 1, send_yc)
    agw[yc] = agz[...]
    wait_in(agw.at[pl.ds(0, NYC - 1)], 3)
    owners = agw[...].reshape(SEQ, WIDTH)
    pick = hot(owners == iota((SEQ, WIDTH), 1).astype(F32))
    grow = hot(iota((HALF, SEQ), 0) // 4 == iota((HALF, SEQ), 1))
    wide = ntdot(dot(grow, pick).astype(BF), grow)
    same = (iota((HALF, HALF), 0) % 4) == (iota((HALF, HALF), 1) % 4)
    q4[...] = jnp.where(same, wide, 0.0).astype(BF)
    tx[...] = dot(q4[...], senc[0:HALF, :]).astype(BF).reshape(SEQ, 4, WIDTH)

    def send_rows(t):
        slot_of, dev = seq_peer(t)
        push(tx.at[slot_of], rx.at[sig], 4, dev)

    loop(SEQ - 1, send_rows)
    rx[sig] = tx[sig]
    c0[...] = dot(q4[...], scot[0:HALF, :]).astype(BF).reshape(NYC, NZ, 4, WIDTH)

    def send_cot(t):
        cc, dev = yc_peer(t)
        push(c0.at[cc], c1.at[yc], 13, dev)

    loop(NYC - 1, send_cot)
    c1[yc] = c0[yc]
    pret[...] = ntdot(pbt[:, 0:HALF], q4[...]).astype(BF)
    patch[HALF:, :] = senc[HALF:, :]
    cotp[HALF:, :] = scot[HALF:, :]
    gain = gain_ref[...]
    gainc = jnp.sum(jnp.where(eye.astype(F32) > 0.5, gain, 0.0), axis=1, keepdims=True)
    wait_in(c1.at[pl.ds(0, NYC - 1)], 13)
    wait_in(rx.at[pl.ds(0, SEQ - 1)], 4)

    def send_cot_z(t):
        zz, dev = z_peer(t)
        push(c1.at[:, zz], c2.at[:, z], 14, dev)

    loop(NZ - 1, send_cot_z)
    c2[:, z] = c1[:, z]
    patch[0:HALF, :] = rx[...].reshape(HALF, WIDTH)

    xT = ntdot(eye, patch[...])
    center = xT - jnp.mean(xT, axis=0, keepdims=True)
    r = lax.rsqrt(jnp.mean(center * center, axis=0, keepdims=True) + 1e-5)
    xh = center * r
    xhT[...] = xh
    rs[...] = jnp.broadcast_to(r, rs.shape)
    nT = (xh * gainc).astype(BF)
    nbT[...] = nT
    mixed = dot(wqT, nT)
    qkvT = mixed.astype(BF)
    qT[...] = qkvT[0:128] * jnp.asarray(0.25, BF)
    kT[...] = qkvT[128:256]
    vT[...] = qkvT[256:384]
    kf[...] = mixed[128:256].T.astype(BF)
    vf[...] = mixed[256:384].T.astype(BF)
    ones = jnp.ones((16, ROWS), BF)
    for h in range(HEADS):
        w1[h * 48 : h * 48 + 16, :] = qkvT[256 + h * 16 : 272 + h * 16]
        w1[h * 48 + 16 : h * 48 + 32, :] = ones
        w1[h * 48 + 32 : h * 48 + 48, :] = qkvT[128 + h * 16 : 144 + h * 16]
    head_of = iota((WIDTH, ROWS), 0) // 16

    def masked(ref, h):
        return jnp.where(head_of == h, ref[...].astype(F32), 0.0).astype(BF)

    first = dot(kf[...], masked(qT, 0))
    sbuf[0] = first
    mref[0] = jnp.broadcast_to(jnp.max(first, axis=0, keepdims=True), (8, ROWS))

    def weighted(h, ks):
        return dot(w1[pl.ds(pl.multiple_of(h * 48, 16), 48), ks], eb[h, ks, :])

    def close(h, a):
        hs = pl.ds(pl.multiple_of(h * 16, 16), 16)
        inv = 1.0 / a[16:17]
        o = a[0:16] * inv
        attT[hs, :] = o.astype(BF)
        oT[hs, :] = o
        keT[hs, :] = a[32:48]
        invs[h] = jnp.broadcast_to(inv, (8, ROWS))

    def forward(h, cur, first, last):
        if not last:
            q_next = masked(qT, h + 1)
        top = mref[cur][0:1, :]
        top_next = None
        a = None
        for c in range(4):
            ks = slice(c * 256, c * 256 + 256)
            if not last:
                s = dot(kf[ks, :], q_next)
                sbuf[1 - cur, ks, :] = s
                high = jnp.max(s, axis=0, keepdims=True)
                top_next = high if top_next is None else jnp.maximum(top_next, high)
            eb[h, ks, :] = jnp.exp(sbuf[cur, ks, :] - top).astype(BF)
            if not first:
                part_a = weighted(h - 1, ks)
                a = part_a if a is None else a + part_a
        if not last:
            mref[1 - cur] = jnp.broadcast_to(top_next, (8, ROWS))
        if not first:
            close(h - 1, a)

    def pair(i, carry):
        forward(2 * i + 1, 1, False, False)
        forward(2 * i + 2, 0, False, False)
        return carry

    forward(0, 0, True, False)
    lax.fori_loop(0, HEADS // 2 - 1, pair, 0)
    forward(HEADS - 1, 1, False, True)
    close(HEADS - 1, weighted(HEADS - 1, slice(0, ROWS)))

    wait_in(c2.at[:, pl.ds(0, NZ - 1)], 14)
    cotp[0:HALF, :] = c2[...].reshape(HALF, WIDTH)
    doT[...] = ntdot(wout_ref[...], cotp[...]).astype(BF)

    def backward(h, cols):
        hs = pl.ds(pl.multiple_of(h * 16, 16), 16)
        inv = invs[h][0:1, :]
        do = doT[hs, :].astype(F32)
        q = qT[hs, :].astype(F32)
        delta = jnp.sum(do * oT[hs, :], axis=0, keepdims=True)
        lead = jnp.concatenate([do * inv, q * (-delta * inv)], axis=0).astype(BF)
        back = ntdot(lead, eb[h, cols, :])
        kx = dot(kT[hs, :], xb[h, :, cols])
        dqT[hs, cols] = ((kx - delta[:, cols] * keT[hs, cols]) * (inv[:, cols] * 0.25)).astype(BF)
        dk = ntdot((q * inv).astype(BF), xb[h, cols, :])
        dvT[hs, cols] = back[0:16].astype(BF)
        dkT[hs, cols] = (dk + back[16:32]).astype(BF)

    def input_grads(cols):
        dall = jnp.concatenate([dqT[:, cols], dkT[:, cols], dvT[:, cols]], axis=0)
        dnT = dot(wq, dall).astype(BF).astype(F32)
        xh = xhT[:, cols]
        dxh = dnT * gainc
        m1 = jnp.mean(dxh, axis=0, keepdims=True)
        m2 = jnp.mean(dxh * xh, axis=0, keepdims=True)
        dxT = (dxh - m1 - xh * m2) * rs[0:1, cols]
        patch[cols, :] = (dxT.T + cotp[cols, :].astype(F32)).astype(BF)
        return jnp.sum(dnT * xh, axis=1, keepdims=True)

    sent = slice(0, HALF)
    kept = slice(HALF, ROWS)

    def back_sent(h, carry):
        do_wide = masked(doT, h)
        for c in range(4):
            ks = slice(c * 256, c * 256 + 256)
            t = dot(vf[ks, :], do_wide)
            xb[h, ks, :] = (eb[h, ks, :].astype(F32) * t).astype(BF)
        backward(h, sent)
        return carry

    def back_kept(h, carry):
        backward(h, kept)
        return carry

    lax.fori_loop(0, HEADS, back_sent, 0)
    ggT = input_grads(sent)
    bt[...] = patch[sent, :].reshape(SEQ, 4, WIDTH)

    def send_back(t):
        slot_of, dev = seq_peer(t)
        push(bt.at[slot_of], rr.at[sig], 5, dev)

    loop(SEQ - 1, send_back)
    rr[sig] = bt[sig]
    lax.fori_loop(0, HEADS, back_kept, 0)
    ggT = ggT + input_grads(kept)

    for j, grad in enumerate((dqT, dkT, dvT)):
        acc[j * 8 : j * 8 + 8] = ntdot(nbT[...], grad[...]).reshape(8, 16, WIDTH)
    acc[24:32] = dot(attT[...], cotp[...]).reshape(8, 16, WIDTH)

    def send_part(t):
        ww, dev = w_peer(t)
        push(acc.at[ww], rsb.at[w], 6, dev)

    loop(NW - 1, send_part)
    rsb[w] = acc[w]
    gain_row = jnp.sum(jnp.where(eye.astype(F32) > 0.5, ggT, 0.0), axis=0, keepdims=True)
    wait_in(rsb.at[pl.ds(0, NW - 1)], 6)
    part[...] = jnp.sum(rsb[...], axis=0)

    def send_part_z(t):
        push(part, zb.at[z], 7, z_peer(t)[1])

    loop(NZ - 1, send_part_z)
    zb[z] = part[...]
    own = dot(pown[...], patch[HALF:, :])

    wait_in(rr.at[pl.ds(0, SEQ - 1)], 5)
    cb = own + dot(pret[...], rr[...].reshape(HALF, WIDTH))
    cpad[8 : 8 + ROWS, :] = cb
    push(cpad.at[pl.ds(ROWS, 8)], cpad.at[pl.ds(0, 8)], 8, nxt)
    push(cpad.at[pl.ds(8, 8)], cpad.at[pl.ds(ROWS + 8, 8)], 9, prv)
    tap_rows = [jnp.sum(cb * pp[5 + t : 5 + t + ROWS, :], axis=0, keepdims=True) for t in range(7)]
    tmine[...] = jnp.concatenate(tap_rows + [gain_row], axis=0)

    def send_tap(t):
        push(tmine, tw.at[w], 10, w_peer(t)[1])

    loop(NW - 1, send_tap)
    tw[w] = tmine[...]
    curve_ref[16 : 16 + ROWS, :] = cb.astype(BF)

    wait_in(tw.at[pl.ds(0, NW - 1)], 10)
    tsum[...] = jnp.sum(tw[...], axis=0)

    def send_tap_z(t):
        push(tsum, tz.at[z], 12, z_peer(t)[1])

    loop(NZ - 1, send_tap_z)
    tz[z] = tsum[...]

    wait_in(zb.at[pl.ds(0, NZ - 1)], 7)
    full[...] = jnp.sum(zb[...], axis=0)

    def send_full(t):
        push(full, fin.at[w], 11, w_peer(t)[1])

    loop(NW - 1, send_full)
    fin[w] = full[...]

    wait_in(cpad.at[pl.ds(0, 8)], 8)
    wait_in(cpad.at[pl.ds(ROWS + 8, 8)], 9)
    wait_out(cpad.at[pl.ds(ROWS, 8)], 8)
    wait_out(cpad.at[pl.ds(8, 8)], 9)
    zero = jnp.zeros((8, WIDTH), F32)
    curve_ref[0:16, :] = jnp.concatenate([zero, cpad[0:8, :] * has_prev], axis=0).astype(BF)
    curve_ref[ROWS + 16 : ROWS + 32, :] = jnp.concatenate(
        [cpad[ROWS + 8 : ROWS + 16, :] * has_next, zero], axis=0
    ).astype(BF)

    wait_out(agz.at[pl.ds(0, NZ - 1)], 0)
    wait_out(agw.at[pl.ds(0, NYC - 1)], 3)
    wait_out(rx.at[pl.ds(0, SEQ - 1)], 4)
    wait_out(c1.at[pl.ds(0, NYC - 1)], 13)
    wait_out(c2.at[:, pl.ds(0, NZ - 1)], 14)
    wait_out(rr.at[pl.ds(0, SEQ - 1)], 5)
    wait_out(rsb.at[pl.ds(0, NW - 1)], 6)
    wait_out(zb.at[pl.ds(0, NZ - 1)], 7)
    wait_out(tw.at[pl.ds(0, NW - 1)], 10)
    wait_out(fin.at[pl.ds(0, NW - 1)], 11)
    wait_out(tz.at[pl.ds(0, NZ - 1)], 12)

    wait_in(fin.at[pl.ds(0, NW - 1)], 11)
    sums_ref[...] = fin[...].reshape(HALF, WIDTH)
    wait_in(tz.at[pl.ds(0, NZ - 1)], 12)
    small_ref[...] = jnp.sum(tz[...], axis=0)


def finish(curve_ref, sums_ref, small_ref, taps_ref, gp_ref, gq_ref, gw_ref, gg_ref, gt_ref, cpad):
    cpad[...] = curve_ref[...].astype(F32)
    res = cpad[16 : 16 + ROWS, :]
    for t in range(7):
        res = res + taps_ref[t : t + 1, :] * cpad[19 - t : 19 - t + ROWS, :]
    gp_ref[0] = res
    for j in range(3):
        gq_ref[:, j * WIDTH : (j + 1) * WIDTH] = sums_ref[j * WIDTH : (j + 1) * WIDTH, :]
    gw_ref[...] = sums_ref[3 * WIDTH :, :]
    gt_ref[...] = small_ref[0:7, :]
    gg_ref[...] = small_ref[7:8, :]


def body(points, grad_rows, order, w_qkv, w_out, norm_gain, conv_taps):
    def vm(shape, dtype):
        return pltpu.VMEM(shape, dtype)

    sq = (ROWS, ROWS)
    wide = (WIDTH, ROWS)
    tall = (ROWS, WIDTH)
    scratch = [
        vm((ROWS + 16, WIDTH), F32), vm((ROWS, HALF), BF), vm((ROWS, HALF), BF), vm((HALF, HALF), BF),
        vm((1, WIDTH), F32), vm((NZ, 1, WIDTH), F32), vm((NYC, NZ, 1, WIDTH), F32), vm(tall, BF), vm(tall, BF),
        vm((SEQ, 4, WIDTH), BF), vm((SEQ, 4, WIDTH), BF),
        vm((NYC, NZ, 4, WIDTH), BF), vm((NYC, NZ, 4, WIDTH), BF), vm((NYC, NZ, 4, WIDTH), BF),
        vm((SEQ, 4, WIDTH), BF), vm((SEQ, 4, WIDTH), BF),
        vm(tall, BF), vm(tall, BF),
        vm(wide, BF), vm(wide, BF), vm(wide, BF), vm(wide, BF), vm(tall, BF), vm(tall, BF),
        vm(wide, BF), vm(wide, BF), vm(wide, BF), vm(wide, BF), vm(wide, F32), vm((8, ROWS), F32), vm(wide, BF),
        vm((2,) + sq, F32), vm((HEADS,) + sq, BF), vm((HEADS,) + sq, BF), vm((HEADS * 48, ROWS), BF), vm((2, 8, ROWS), F32),
        vm(wide, F32), vm(wide, F32), vm((HEADS, 8, ROWS), F32),
        vm((ROWS + 16, WIDTH), F32), vm((NW, 16, WIDTH), F32), vm((NW, 16, WIDTH), F32), vm((16, WIDTH), F32),
        vm((NZ, 16, WIDTH), F32), vm((16, WIDTH), F32), vm((NW, 16, WIDTH), F32),
        vm((8, WIDTH), F32), vm((NW, 8, WIDTH), F32), vm((8, WIDTH), F32), vm((NZ, 8, WIDTH), F32),
        pltpu.SemaphoreType.DMA((15,)), pltpu.SemaphoreType.DMA((15,)),
    ]
    spec = pl.BlockSpec(memory_space=pltpu.VMEM)
    shape = jax.ShapeDtypeStruct
    curve, sums, small = pl.pallas_call(
        kernel,
        out_shape=(shape((ROWS + 32, WIDTH), BF), shape((HALF, WIDTH), F32), shape((8, WIDTH), F32)),
        in_specs=[spec] * 7,
        out_specs=[spec] * 3,
        scratch_shapes=scratch,
        compiler_params=pltpu.CompilerParams(
            collective_id=0, has_side_effects=True, vmem_limit_bytes=60 * 2**20
        ),
    )(points, grad_rows, order, w_qkv, w_out, norm_gain.reshape(1, WIDTH), conv_taps)
    gp, gq, gw, gg, gt = pl.pallas_call(
        finish,
        out_shape=(
            shape((1, ROWS, WIDTH), F32), shape((WIDTH, 3 * WIDTH), F32), shape((WIDTH, WIDTH), F32),
            shape((1, WIDTH), F32), shape((7, WIDTH), F32),
        ),
        in_specs=[spec] * 4,
        out_specs=[spec] * 5,
        scratch_shapes=[vm((ROWS + 32, WIDTH), F32)],
    )(curve, sums, small, conv_taps)
    return gp, gq, gw, gg.reshape(WIDTH), gt


def solution(mesh):
    placed = (P("rep", "seq", None), P("rep", "seq", None), P("rep", "seq"), P(), P(), P(), P())
    return jax.shard_map(
        body,
        mesh=mesh,
        in_specs=placed,
        out_specs=(P("rep", "seq", None), P(), P(), P(), P()),
        check_vma=False,
    )
```

```python
import functools

import jax
import jax.numpy as jnp
from jax import lax
from jax.experimental import pallas as pl
from jax.experimental.pallas import tpu as pltpu
from jax.sharding import PartitionSpec as P

F32 = jnp.float32
BF = jnp.bfloat16
MESH = pl.DeviceIdType.MESH
HEADS = 8
HALF = 512
ROWS = 1024
WIDTH = 128
NZ = 16
NYC = 8
NX = 4
NW = NX * NYC
SEQ = NZ * NYC


def dot(a, b):
    return jnp.dot(a, b, preferred_element_type=F32)


def ntdot(a, b):
    return lax.dot_general(a, b, (((1,), (1,)), ((), ())), preferred_element_type=F32)


def iota(shape, dim):
    return lax.broadcasted_iota(jnp.int32, shape, dim)


def hot(cond):
    return jnp.where(cond, 1.0, 0.0).astype(BF)


def kernel(
    pts_ref, cot_ref, order_ref, wqkv_ref, wout_ref, gain_ref, taps_ref,
    curve_ref, sums_ref, small_ref,
    pp, pown, pret, q4, mine, agz, agw, scot, senc,
    tx, rx, c0, c1, c2, bt, rr, patch, cotp,
    qT, kT, vT, doT, kf, vf, attT, dqT, dkT, dvT, xhT, rs, nbT, sbuf, eb, xb, w1, mref,
    oT, keT, invs,
    cpad, acc, rsb, part, zb, full, fin, tmine, tw, tsum, tz,
    ssem, rsem,
):
    me = lax.axis_index("seq")
    rep = lax.axis_index("rep")
    z = me // NYC
    yc = lax.rem(me, NYC)
    w = rep * NYC + yc
    sig = yc * NZ + z

    def z_peer(t):
        zz = lax.rem(z + 1 + t, NZ)
        return zz, (zz * NYC + yc, rep)

    def yc_peer(t):
        cc = lax.rem(yc + 1 + t, NYC)
        return cc, (z * NYC + cc, rep)

    def w_peer(t):
        ww = lax.rem(w + 1 + t, NW)
        return ww, (z * NYC + lax.rem(ww, NYC), ww // NYC)

    def seq_peer(t):
        dd = lax.rem(me + 1 + t, SEQ)
        return lax.rem(dd, NYC) * NZ + dd // NYC, (dd, rep)

    nxt = (lax.rem(me + 1, SEQ), rep)
    prv = (lax.rem(me + SEQ - 1, SEQ), rep)

    def push(src, dst, k, dev):
        pltpu.make_async_remote_copy(
            src_ref=src, dst_ref=dst, send_sem=ssem.at[k], recv_sem=rsem.at[k],
            device_id=dev, device_id_type=MESH,
        ).start()

    def loop(count, step):
        def body(t, carry):
            step(t)
            return carry

        lax.fori_loop(0, count, body, 0)

    def wait_in(ref, k):
        pltpu.make_async_copy(ref, ref, rsem.at[k]).wait()

    def wait_out(ref, k):
        pltpu.make_async_copy(ref, ref, ssem.at[k]).wait()

    barrier = pltpu.get_barrier_semaphore()
    sent = slice(0, HALF)
    kept = slice(HALF, ROWS)
    pb = xb.at[0]
    pbt = xb.at[1]

    def greet(dev):
        pl.semaphore_signal(barrier, inc=1, device_id=dev, device_id_type=MESH)

    loop(NZ - 1, lambda t: greet(z_peer(t)[1]))
    loop(NYC - 1, lambda t: greet(yc_peer(t)[1]))
    loop(NX - 1, lambda t: greet((me, lax.rem(rep + 1 + t, NX))))
    greet(nxt)
    greet(prv)

    pp[8 : 8 + ROWS, :] = pts_ref[0].astype(F32)
    dest = order_ref[...] // ROWS
    blocks = iota((SEQ, ROWS), 0)
    hits = jnp.where(blocks == dest, 1.0, 0.0)
    counts = jnp.sum(hits, axis=1, keepdims=True)
    is_main = jnp.where(counts > 4.5, 1.0, 0.0)
    main = jnp.sum(is_main * iota((SEQ, 1), 0).astype(F32), axis=0, keepdims=True)
    mine[...] = jnp.broadcast_to(main, (1, WIDTH))
    pb[...] = hot(iota((ROWS, ROWS), 0) < iota((ROWS, ROWS), 1))
    before = dot(hits.astype(BF), pb[...])
    rank = jnp.sum(hits * before, axis=0, keepdims=True)
    main_row = jnp.sum(hits * is_main, axis=0, keepdims=True)
    slot = jnp.where(
        (main_row > 0.5) & (rank > 3.5),
        rank + float(HALF - 4),
        dest.astype(F32) * 4.0 + rank,
    )
    pb[...] = hot(iota((ROWS, ROWS), 0).astype(F32) == slot)
    slot_col = jnp.broadcast_to(slot, (8, ROWS)).T[:, 0:1]
    pbt[...] = hot(iota((ROWS, ROWS), 1).astype(F32) == slot_col)
    pown[...] = pbt[:, HALF:]
    scot[...] = dot(pb[...], cot_ref[0]).astype(BF)
    eye = hot(iota((WIDTH, WIDTH), 0) == iota((WIDTH, WIDTH), 1))
    wq = wqkv_ref[...]
    wqT = jnp.concatenate(
        [wq[:, j * WIDTH : (j + 1) * WIDTH].astype(F32).T.astype(BF) for j in range(3)], axis=0
    )

    pl.semaphore_wait(barrier, NZ - 1 + NYC - 1 + NX - 1 + 2)

    def send_z(t):
        push(mine, agz.at[z], 0, z_peer(t)[1])

    loop(NZ - 1, send_z)
    push(pp.at[pl.ds(ROWS, 8)], pp.at[pl.ds(0, 8)], 1, nxt)
    push(pp.at[pl.ds(8, 8)], pp.at[pl.ds(ROWS + 8, 8)], 2, prv)
    agz[z] = mine[...]
    wait_in(pp.at[pl.ds(0, 8)], 1)
    wait_in(pp.at[pl.ds(ROWS + 8, 8)], 2)
    has_prev = jnp.where(me > 0, 1.0, 0.0)
    has_next = jnp.where(me < SEQ - 1, 1.0, 0.0)
    wait_out(pp.at[pl.ds(ROWS, 8)], 1)
    wait_out(pp.at[pl.ds(8, 8)], 2)
    pp[0:8, :] = pp[0:8, :] * has_prev
    pp[ROWS + 8 : ROWS + 16, :] = pp[ROWS + 8 : ROWS + 16, :] * has_next
    enc = pp[8 : 8 + ROWS, :]
    for t in range(7):
        enc = enc + taps_ref[t : t + 1, :] * pp[5 + t : 5 + t + ROWS, :]
    senc[...] = dot(pb[...], enc.astype(BF)).astype(BF)
    wait_in(agz.at[pl.ds(0, NZ - 1)], 0)

    def send_yc(t):
        push(agz, agw.at[yc], 3, yc_peer(t)[1])

    loop(NYC - 1, send_yc)
    agw[yc] = agz[...]
    wait_in(agw.at[pl.ds(0, NYC - 1)], 3)
    owners = agw[...].reshape(SEQ, WIDTH)
    pick = hot(owners == iota((SEQ, WIDTH), 1).astype(F32))
    grow = hot(iota((HALF, SEQ), 0) // 4 == iota((HALF, SEQ), 1))
    wide = ntdot(dot(grow, pick).astype(BF), grow)
    same = (iota((HALF, HALF), 0) % 4) == (iota((HALF, HALF), 1) % 4)
    q4[...] = jnp.where(same, wide, 0.0).astype(BF)
    tx[...] = dot(q4[...], senc[0:HALF, :]).astype(BF).reshape(SEQ, 4, WIDTH)

    def send_rows(t):
        slot_of, dev = seq_peer(t)
        push(tx.at[slot_of], rx.at[sig], 4, dev)

    loop(SEQ - 1, send_rows)
    rx[sig] = tx[sig]
    c0[...] = dot(q4[...], scot[0:HALF, :]).astype(BF).reshape(NYC, NZ, 4, WIDTH)

    def send_cot(t):
        cc, dev = yc_peer(t)
        push(c0.at[cc], c1.at[yc], 13, dev)

    loop(NYC - 1, send_cot)
    c1[yc] = c0[yc]
    pret[...] = ntdot(pbt[:, 0:HALF], q4[...]).astype(BF)
    patch[HALF:, :] = senc[HALF:, :]
    cotp[HALF:, :] = scot[HALF:, :]
    def project(cols):
        xT = ntdot(eye, patch[cols, :])
        center = xT - jnp.mean(xT, axis=0, keepdims=True)
        r = lax.rsqrt(jnp.mean(center * center, axis=0, keepdims=True) + 1e-5)
        xh = center * r
        xhT[:, cols] = xh
        rs[:, cols] = jnp.broadcast_to(r, (8, HALF))
        nT = (xh * gainc).astype(BF)
        nbT[:, cols] = nT
        mixed = dot(wqT, nT)
        qkvT = mixed.astype(BF)
        qT[:, cols] = qkvT[0:128] * jnp.asarray(0.25, BF)
        kT[:, cols] = qkvT[128:256]
        vT[:, cols] = qkvT[256:384]
        kf[cols, :] = mixed[128:256].T.astype(BF)
        vf[cols, :] = mixed[256:384].T.astype(BF)
        for h in range(HEADS):
            w1[h * 48 : h * 48 + 16, cols] = qkvT[256 + h * 16 : 272 + h * 16]
            w1[h * 48 + 16 : h * 48 + 32, cols] = jnp.ones((16, HALF), BF)
            w1[h * 48 + 32 : h * 48 + 48, cols] = qkvT[128 + h * 16 : 144 + h * 16]

    gain = gain_ref[...]
    gainc = jnp.sum(jnp.where(eye.astype(F32) > 0.5, gain, 0.0), axis=1, keepdims=True)
    project(kept)
    wait_in(c1.at[pl.ds(0, NYC - 1)], 13)

    def send_cot_z(t):
        zz, dev = z_peer(t)
        push(c1.at[:, zz], c2.at[:, z], 14, dev)

    loop(NZ - 1, send_cot_z)
    c2[:, z] = c1[:, z]
    wait_in(rx.at[pl.ds(0, SEQ - 1)], 4)
    patch[0:HALF, :] = rx[...].reshape(HALF, WIDTH)
    project(sent)

    head_of = iota((WIDTH, ROWS), 0) // 16

    def masked(ref, h):
        return jnp.where(head_of == h, ref[...].astype(F32), 0.0).astype(BF)

    first = dot(kf[...], masked(qT, 0))
    sbuf[0] = first
    mref[0] = jnp.broadcast_to(jnp.max(first, axis=0, keepdims=True), (8, ROWS))

    def weighted(h, ks):
        return dot(w1[pl.ds(pl.multiple_of(h * 48, 16), 48), ks], eb[h, ks, :])

    def close(h, a):
        hs = pl.ds(pl.multiple_of(h * 16, 16), 16)
        inv = 1.0 / a[16:17]
        o = a[0:16] * inv
        attT[hs, :] = o.astype(BF)
        oT[hs, :] = o
        keT[hs, :] = a[32:48]
        invs[h] = jnp.broadcast_to(inv, (8, ROWS))

    def forward(h, cur, first, last):
        if not last:
            q_next = masked(qT, h + 1)
        top = mref[cur][0:1, :]
        top_next = None
        a = None
        for c in range(4):
            ks = slice(c * 256, c * 256 + 256)
            if not last:
                s = dot(kf[ks, :], q_next)
                sbuf[1 - cur, ks, :] = s
                high = jnp.max(s, axis=0, keepdims=True)
                top_next = high if top_next is None else jnp.maximum(top_next, high)
            eb[h, ks, :] = jnp.exp(sbuf[cur, ks, :] - top).astype(BF)
            if not first:
                part_a = weighted(h - 1, ks)
                a = part_a if a is None else a + part_a
        if not last:
            mref[1 - cur] = jnp.broadcast_to(top_next, (8, ROWS))
        if not first:
            close(h - 1, a)

    def pair(i, carry):
        forward(2 * i + 1, 1, False, False)
        forward(2 * i + 2, 0, False, False)
        return carry

    forward(0, 0, True, False)
    lax.fori_loop(0, HEADS // 2 - 1, pair, 0)
    forward(HEADS - 1, 1, False, True)
    close(HEADS - 1, weighted(HEADS - 1, slice(0, ROWS)))

    wait_in(c2.at[:, pl.ds(0, NZ - 1)], 14)
    cotp[0:HALF, :] = c2[...].reshape(HALF, WIDTH)
    doT[...] = ntdot(wout_ref[...], cotp[...]).astype(BF)

    def backward(h, cols):
        hs = pl.ds(pl.multiple_of(h * 16, 16), 16)
        inv = invs[h][0:1, :]
        do = doT[hs, :].astype(F32)
        q = qT[hs, :].astype(F32)
        delta = jnp.sum(do * oT[hs, :], axis=0, keepdims=True)
        lead = jnp.concatenate([do * inv, q * (-delta * inv)], axis=0).astype(BF)
        back = ntdot(lead, eb[h, cols, :])
        kx = dot(kT[hs, :], xb[h, :, cols])
        dqT[hs, cols] = ((kx - delta[:, cols] * keT[hs, cols]) * (inv[:, cols] * 0.25)).astype(BF)
        dk = ntdot((q * inv).astype(BF), xb[h, cols, :])
        dvT[hs, cols] = back[0:16].astype(BF)
        dkT[hs, cols] = (dk + back[16:32]).astype(BF)

    def input_grads(cols):
        dall = jnp.concatenate([dqT[:, cols], dkT[:, cols], dvT[:, cols]], axis=0)
        dnT = dot(wq, dall).astype(BF).astype(F32)
        xh = xhT[:, cols]
        dxh = dnT * gainc
        m1 = jnp.mean(dxh, axis=0, keepdims=True)
        m2 = jnp.mean(dxh * xh, axis=0, keepdims=True)
        dxT = (dxh - m1 - xh * m2) * rs[0:1, cols]
        patch[cols, :] = (dxT.T + cotp[cols, :].astype(F32)).astype(BF)
        return jnp.sum(dnT * xh, axis=1, keepdims=True)

    def back_sent(h, carry):
        do_wide = masked(doT, h)
        for c in range(4):
            ks = slice(c * 256, c * 256 + 256)
            cols = slice(0, ROWS) if c < 2 else sent
            t = dot(vf[ks, :], do_wide[:, cols])
            xb[h, ks, cols] = (eb[h, ks, cols].astype(F32) * t).astype(BF)
        backward(h, sent)
        return carry

    def back_kept(h, carry):
        do_wide = masked(doT, h)[:, kept]
        for c in range(2, 4):
            ks = slice(c * 256, c * 256 + 256)
            t = dot(vf[ks, :], do_wide)
            xb[h, ks, kept] = (eb[h, ks, kept].astype(F32) * t).astype(BF)
        backward(h, kept)
        return carry

    lax.fori_loop(0, HEADS, back_sent, 0)
    ggT = input_grads(sent)
    bt[...] = patch[sent, :].reshape(SEQ, 4, WIDTH)

    def send_back(t):
        slot_of, dev = seq_peer(t)
        push(bt.at[slot_of], rr.at[sig], 5, dev)

    loop(SEQ - 1, send_back)
    rr[sig] = bt[sig]
    lax.fori_loop(0, HEADS, back_kept, 0)
    ggT = ggT + input_grads(kept)

    for j, grad in enumerate((dqT, dkT, dvT)):
        acc[j * 8 : j * 8 + 8] = ntdot(nbT[...], grad[...]).astype(BF).reshape(8, 16, WIDTH)
    acc[24:32] = dot(attT[...], cotp[...]).astype(BF).reshape(8, 16, WIDTH)

    def send_part(t):
        ww, dev = w_peer(t)
        push(acc.at[ww], rsb.at[w], 6, dev)

    loop(NW - 1, send_part)
    rsb[w] = acc[w]
    gain_row = jnp.sum(jnp.where(eye.astype(F32) > 0.5, ggT, 0.0), axis=0, keepdims=True)
    wait_in(rsb.at[pl.ds(0, NW - 1)], 6)
    part[...] = jnp.sum(rsb[...].astype(F32), axis=0).astype(BF)

    def send_part_z(t):
        push(part, zb.at[z], 7, z_peer(t)[1])

    loop(NZ - 1, send_part_z)
    zb[z] = part[...]
    own = dot(pown[...], patch[HALF:, :])

    wait_in(rr.at[pl.ds(0, SEQ - 1)], 5)
    cb = own + dot(pret[...], rr[...].reshape(HALF, WIDTH))
    cpad[8 : 8 + ROWS, :] = cb
    push(cpad.at[pl.ds(ROWS, 8)], cpad.at[pl.ds(0, 8)], 8, nxt)
    push(cpad.at[pl.ds(8, 8)], cpad.at[pl.ds(ROWS + 8, 8)], 9, prv)
    tap_rows = [jnp.sum(cb * pp[5 + t : 5 + t + ROWS, :], axis=0, keepdims=True) for t in range(7)]
    tmine[...] = jnp.concatenate(tap_rows + [gain_row], axis=0)

    def send_tap(t):
        push(tmine, tw.at[w], 10, w_peer(t)[1])

    loop(NW - 1, send_tap)
    tw[w] = tmine[...]
    curve_ref[16 : 16 + ROWS, :] = cb.astype(BF)

    wait_in(tw.at[pl.ds(0, NW - 1)], 10)
    tsum[...] = jnp.sum(tw[...], axis=0)

    def send_tap_z(t):
        push(tsum, tz.at[z], 12, z_peer(t)[1])

    loop(NZ - 1, send_tap_z)
    tz[z] = tsum[...]

    wait_in(zb.at[pl.ds(0, NZ - 1)], 7)
    full[...] = jnp.sum(zb[...].astype(F32), axis=0)

    def send_full(t):
        push(full, fin.at[w], 11, w_peer(t)[1])

    loop(NW - 1, send_full)
    fin[w] = full[...]

    wait_in(cpad.at[pl.ds(0, 8)], 8)
    wait_in(cpad.at[pl.ds(ROWS + 8, 8)], 9)
    wait_out(cpad.at[pl.ds(ROWS, 8)], 8)
    wait_out(cpad.at[pl.ds(8, 8)], 9)
    zero = jnp.zeros((8, WIDTH), F32)
    curve_ref[0:16, :] = jnp.concatenate([zero, cpad[0:8, :] * has_prev], axis=0).astype(BF)
    curve_ref[ROWS + 16 : ROWS + 32, :] = jnp.concatenate(
        [cpad[ROWS + 8 : ROWS + 16, :] * has_next, zero], axis=0
    ).astype(BF)

    wait_out(agz.at[pl.ds(0, NZ - 1)], 0)
    wait_out(agw.at[pl.ds(0, NYC - 1)], 3)
    wait_out(rx.at[pl.ds(0, SEQ - 1)], 4)
    wait_out(c1.at[pl.ds(0, NYC - 1)], 13)
    wait_out(c2.at[:, pl.ds(0, NZ - 1)], 14)
    wait_out(rr.at[pl.ds(0, SEQ - 1)], 5)
    wait_out(rsb.at[pl.ds(0, NW - 1)], 6)
    wait_out(zb.at[pl.ds(0, NZ - 1)], 7)
    wait_out(tw.at[pl.ds(0, NW - 1)], 10)
    wait_out(fin.at[pl.ds(0, NW - 1)], 11)
    wait_out(tz.at[pl.ds(0, NZ - 1)], 12)

    wait_in(fin.at[pl.ds(0, NW - 1)], 11)
    sums_ref[...] = fin[...].reshape(HALF, WIDTH)
    wait_in(tz.at[pl.ds(0, NZ - 1)], 12)
    small_ref[...] = jnp.sum(tz[...], axis=0)


def finish(curve_ref, sums_ref, small_ref, taps_ref, gp_ref, gq_ref, gw_ref, gg_ref, gt_ref, cpad):
    cpad[...] = curve_ref[...].astype(F32)
    res = cpad[16 : 16 + ROWS, :]
    for t in range(7):
        res = res + taps_ref[t : t + 1, :] * cpad[19 - t : 19 - t + ROWS, :]
    gp_ref[0] = res
    for j in range(3):
        gq_ref[:, j * WIDTH : (j + 1) * WIDTH] = sums_ref[j * WIDTH : (j + 1) * WIDTH, :]
    gw_ref[...] = sums_ref[3 * WIDTH :, :]
    gt_ref[...] = small_ref[0:7, :]
    gg_ref[...] = small_ref[7:8, :]


def body(points, grad_rows, order, w_qkv, w_out, norm_gain, conv_taps):
    def vm(shape, dtype):
        return pltpu.VMEM(shape, dtype)

    sq = (ROWS, ROWS)
    wide = (WIDTH, ROWS)
    tall = (ROWS, WIDTH)
    scratch = [
        vm((ROWS + 16, WIDTH), F32), vm((ROWS, HALF), BF), vm((ROWS, HALF), BF), vm((HALF, HALF), BF),
        vm((1, WIDTH), F32), vm((NZ, 1, WIDTH), F32), vm((NYC, NZ, 1, WIDTH), F32), vm(tall, BF), vm(tall, BF),
        vm((SEQ, 4, WIDTH), BF), vm((SEQ, 4, WIDTH), BF),
        vm((NYC, NZ, 4, WIDTH), BF), vm((NYC, NZ, 4, WIDTH), BF), vm((NYC, NZ, 4, WIDTH), BF),
        vm((SEQ, 4, WIDTH), BF), vm((SEQ, 4, WIDTH), BF),
        vm(tall, BF), vm(tall, BF),
        vm(wide, BF), vm(wide, BF), vm(wide, BF), vm(wide, BF), vm(tall, BF), vm(tall, BF),
        vm(wide, BF), vm(wide, BF), vm(wide, BF), vm(wide, BF), vm(wide, F32), vm((8, ROWS), F32), vm(wide, BF),
        vm((2,) + sq, F32), vm((HEADS,) + sq, BF), vm((HEADS,) + sq, BF), vm((HEADS * 48, ROWS), BF), vm((2, 8, ROWS), F32),
        vm(wide, F32), vm(wide, F32), vm((HEADS, 8, ROWS), F32),
        vm((ROWS + 16, WIDTH), F32), vm((NW, 16, WIDTH), BF), vm((NW, 16, WIDTH), BF), vm((16, WIDTH), BF),
        vm((NZ, 16, WIDTH), BF), vm((16, WIDTH), F32), vm((NW, 16, WIDTH), F32),
        vm((8, WIDTH), F32), vm((NW, 8, WIDTH), F32), vm((8, WIDTH), F32), vm((NZ, 8, WIDTH), F32),
        pltpu.SemaphoreType.DMA((15,)), pltpu.SemaphoreType.DMA((15,)),
    ]
    spec = pl.BlockSpec(memory_space=pltpu.VMEM)
    shape = jax.ShapeDtypeStruct
    curve, sums, small = pl.pallas_call(
        kernel,
        out_shape=(shape((ROWS + 32, WIDTH), BF), shape((HALF, WIDTH), F32), shape((8, WIDTH), F32)),
        in_specs=[spec] * 7,
        out_specs=[spec] * 3,
        scratch_shapes=scratch,
        compiler_params=pltpu.CompilerParams(
            collective_id=0, has_side_effects=True, vmem_limit_bytes=60 * 2**20
        ),
    )(points, grad_rows, order, w_qkv, w_out, norm_gain.reshape(1, WIDTH), conv_taps)
    gp, gq, gw, gg, gt = pl.pallas_call(
        finish,
        out_shape=(
            shape((1, ROWS, WIDTH), F32), shape((WIDTH, 3 * WIDTH), F32), shape((WIDTH, WIDTH), F32),
            shape((1, WIDTH), F32), shape((7, WIDTH), F32),
        ),
        in_specs=[spec] * 4,
        out_specs=[spec] * 5,
        scratch_shapes=[vm((ROWS + 32, WIDTH), F32)],
    )(curve, sums, small, conv_taps)
    return gp, gq, gw, gg.reshape(WIDTH), gt


def solution(mesh):
    placed = (P("rep", "seq", None), P("rep", "seq", None), P("rep", "seq"), P(), P(), P(), P())
    return jax.shard_map(
        body,
        mesh=mesh,
        in_specs=placed,
        out_specs=(P("rep", "seq", None), P(), P(), P(), P()),
        check_vma=False,
    )
```
